256 devices in a mesh: row: 4 (over z_lo, core), col: 16 (over x, y), chan: 4 (over z_hi).
Axes of the slice: x: 4, y: 4, z: 8 (z_hi: 4, z_lo: 2; z = z_hi * 2 + z_lo), core: 2. Of those that a mesh axis runs over, the one named last changes fastest.
Arguments:
- pair: bfloat16 [1024, 1024, 128], P('row', 'col'), may hold values from -6 to 6
- pair_mask: int32 [1024, 1024], P('row', 'col'), may hold values 0 or 1
- ln_gain: float32 [128], replicated, may hold values from 0.1 to 1.9
- ln_bias: float32 [128], replicated, may hold values from -3 to 3
- left_value: bfloat16 [128, 128], P(None, 'chan'), may hold values from -0.5 to 0.5
- left_gate: bfloat16 [128, 128], P(None, 'chan'), may hold values from -0.5 to 0.5
- right_value: bfloat16 [128, 128], P(None, 'chan'), may hold values from -0.5 to 0.5
- right_gate: bfloat16 [128, 128], P(None, 'chan'), may hold values from -0.5 to 0.5
- hid_gain: float32 [128], replicated, may hold values from 0.1 to 1.9
- hid_bias: float32 [128], replicated, may hold values from -3 to 3
- out_weight: bfloat16 [128, 128], replicated, may hold values from -0.5 to 0.5
- out_gate: bfloat16 [128, 128], replicated, may hold values from -0.5 to 0.5
Outputs:
- update: bfloat16 [1024, 1024, 128], P('row', ('col', 'chan'))
The draws below stay inside these ranges and needn't reach their ends.
All inputs are finite; a program needn't handle non-finite values. No bound on the sum of `pair_mask` on one device may be relied on, other than what follows from the above.
Results may differ from the reference program's by a relative error of at most 0.025.
Values may be sent and summed in bfloat16 or wider, within the bound.
No kernel may reach another device: no remote copies, remote signals or barrier semaphores. Data moves between devices by JAX's collectives and lax.ppermute only.
A program may use at most 128 MiB of HBM per device.

```python
import jax
import jax.numpy as jnp
from jax import lax

C = 128
HID = 128
N = 1024


def set_ends(drawn, rng, smallest, largest):
    spot = [jax.random.randint(jax.random.fold_in(rng, axis), (), 0, length) for axis, length in enumerate(drawn.shape)]
    main_axis = drawn.shape.index(max(drawn.shape))
    beside = spot[:main_axis] + [(spot[main_axis] + 1) % drawn.shape[main_axis]] + spot[main_axis + 1:]
    return drawn.at[tuple(spot)].set(smallest).at[tuple(beside)].set(largest)


def shard_levels(stream_key, shape, shards, least, top_value):
    level, own = 1.0, jax.random.fold_in(stream_key, 6)
    for dim, parts in shards:
        steps = jnp.exp(jax.random.uniform(jax.random.fold_in(own, dim), (parts,), jnp.float32, least / len(shards), top_value / len(shards)))
        level = level * jnp.repeat(steps, shape[dim] // parts).reshape([-1 if axis == dim else 1 for axis in range(len(shape))])
    return level


def scatter_about(own_key, shape, scale, bound, shards=(), held_as=jnp.bfloat16):
    gain = shard_levels(own_key, shape, shards, -0.22, 0.18) if shards else 1.0
    values = jax.random.normal(own_key, shape, jnp.float32) * scale * gain
    return jnp.minimum(jnp.maximum(values, -bound), bound).astype(held_as)


def setup_inputs(seed: int = 0) -> dict:
    seeds = jax.random.split(jax.random.key(seed), 13)
    return {
        "pair": scatter_about(seeds[0], (N, N, C), 1.0, 6.0, ((0, 4), (1, 16))),
        "pair_mask": set_ends((jax.random.randint(seeds[1], (N, N), 0, 4) < 3).astype(jnp.int32), jax.random.fold_in(seeds[1], 1), 0, 1),
        "ln_gain": jnp.clip(1.0 + 0.18 * jax.random.normal(seeds[2], (C,), jnp.float32), 0.1, 1.9),
        "ln_bias": scatter_about(seeds[3], (C,), 0.5, 3.0, (), jnp.float32),
        "left_value": scatter_about(seeds[4], (C, HID), C ** -0.5, 0.5, ((1, 4),)),
        "left_gate": scatter_about(seeds[5], (C, HID), C ** -0.5, 0.5, ((1, 4),)),
        "right_value": scatter_about(seeds[6], (C, HID), C ** -0.5, 0.5, ((1, 4),)),
        "right_gate": scatter_about(seeds[7], (C, HID), C ** -0.5, 0.5, ((1, 4),)),
        "hid_gain": jnp.clip(1.0 + 0.18 * jax.random.normal(seeds[8], (HID,), jnp.float32), 0.1, 1.9),
        "hid_bias": scatter_about(seeds[9], (HID,), 0.5, 3.0, (), jnp.float32),
        "out_weight": scatter_about(seeds[10], (HID, C), HID ** -0.5, 0.5),
        "out_gate": scatter_about(seeds[11], (C, C), C ** -0.5, 0.5),
    }


def widen(values):
    return lax.optimization_barrier(values).astype(jnp.float32)

def reference(pair, pair_mask, ln_gain, ln_bias, left_value, left_gate, right_value, right_gate, hid_gain, hid_bias, out_weight, out_gate):
    source = pair.astype(jnp.float32)
    centre = lax.optimization_barrier(jnp.mean(source, axis=-1, keepdims=True))
    shifted = source - centre
    spread = lax.optimization_barrier(jnp.mean(shifted * shifted, axis=-1, keepdims=True))
    normed = (shifted * lax.rsqrt(spread + 1e-05) * ln_gain + ln_bias).astype(jnp.bfloat16)
    normed_wide = widen(normed)
    valid = pair_mask.astype(jnp.float32)[:, :, None]

    def project(weight):
        return jnp.einsum('ikc,ch->ikh', normed_wide, weight.astype(jnp.float32))
    left = (jax.nn.sigmoid(project(left_gate)) * project(left_value) * valid).astype(jnp.bfloat16)
    right = (jax.nn.sigmoid(project(right_gate)) * project(right_value) * valid).astype(jnp.bfloat16)
    product = jnp.einsum('ikh,jkh->ijh', widen(left), widen(right)).astype(jnp.bfloat16)
    widened = widen(product)
    mean_hid = lax.optimization_barrier(jnp.mean(widened, axis=-1, keepdims=True))
    spread_hid = lax.optimization_barrier(jnp.mean(widened * widened, axis=-1, keepdims=True)) - mean_hid * mean_hid
    hidden = ((widened - mean_hid) * lax.rsqrt(spread_hid + 1e-05) * hid_gain + hid_bias).astype(jnp.bfloat16)
    mixed = jnp.einsum('ijh,hc->ijc', widen(hidden), out_weight.astype(jnp.float32))
    gating = jax.nn.sigmoid(jnp.einsum('ijc,cd->ijd', normed_wide, out_gate.astype(jnp.float32)))
    return (gating * mixed).astype(jnp.bfloat16)
```

```python
import jax
import jax.numpy as jnp
from jax import lax
from jax.experimental import pallas as pl
from jax.experimental.pallas import tpu as pltpu
from jax.sharding import Mesh, PartitionSpec as P

F32 = jnp.float32
BF16 = jnp.bfloat16
EPS = 1e-05
VMEM_LIMIT = 48 * 1024 * 1024

TILE_I = 256
TILE_K = 64
CH = 128
GROUP = 32
KB = 16


def gate(x):
    return 0.5 * jnp.tanh(0.5 * x) + 0.5


def layer_norm(x, gain, bias):
    centre = jnp.mean(x, axis=-1, keepdims=True)
    shifted = x - centre
    spread = jnp.mean(shifted * shifted, axis=-1, keepdims=True)
    return shifted * lax.rsqrt(spread + EPS) * gain + bias


def project_kernel(
    pair_ref, mask_ref, gain_ref, bias_ref, lv_ref, lg_ref, rv_ref, rg_ref,
    out_ref, weights, valid, normed, staged,
):
    step = pl.program_id(0)

    @pl.when(step == 0)
    def _():
        joined = jnp.concatenate(
            [lv_ref[...], rv_ref[...], lg_ref[...], rg_ref[...]], axis=1
        ).astype(F32)
        weights[...] = joined.T.astype(BF16)
        rows = lax.broadcasted_iota(jnp.int32, (TILE_K, TILE_K), 0)
        cols = lax.broadcasted_iota(jnp.int32, (TILE_K, TILE_K), 1)
        same = jnp.where(rows == cols, 1.0, 0.0).astype(BF16)
        valid[...] = lax.dot_general(
            same, mask_ref[...].astype(F32).astype(BF16),
            (((1,), (1,)), ((), ())), preferred_element_type=F32,
        )

    gain = gain_ref[...].reshape(1, 1, CH)
    bias = bias_ref[...].reshape(1, 1, CH)
    batch = 16

    @pl.loop(0, TILE_I // batch)
    def _(part):
        x = pair_ref[pl.ds(part * batch, batch)].astype(F32)
        n = layer_norm(x, gain, bias)
        normed[pl.ds(part * batch * KB, batch * KB), :] = n.reshape(batch * KB, CH)

    for k in range(KB):
        rows = normed[pl.ds(k, TILE_I, stride=KB), :].astype(BF16)
        y = lax.dot_general(
            weights[...], rows, (((1,), (1,)), ((), ())), preferred_element_type=F32
        )
        kept = valid[pl.ds(step * KB + k, 1), :]
        both = gate(y[2 * GROUP :]) * y[: 2 * GROUP] * kept
        for part in range(2):
            staged[part, pl.ds(k, 2 * GROUP, stride=KB), :] = both[:, part * 128 : (part + 1) * 128]

    for side in range(2):
        for part in range(2):
            block = staged[part, pl.ds(side * GROUP * KB, GROUP * KB), :]
            out_ref[:, side, :, part * 128 : (part + 1) * 128] = block.reshape(GROUP, KB, 128).astype(BF16)


def project(pair, mask, gain, bias, lv, lg, rv, rg):
    whole = lambda *shape: pl.BlockSpec(shape, lambda s: (0,) * len(shape))
    return pl.pallas_call(
        project_kernel,
        grid=(TILE_K // KB,),
        in_specs=[
            pl.BlockSpec((TILE_I, KB, CH), lambda s: (0, s, 0)),
            whole(TILE_I, TILE_K),
            whole(1, CH),
            whole(1, CH),
            whole(CH, GROUP),
            whole(CH, GROUP),
            whole(CH, GROUP),
            whole(CH, GROUP),
        ],
        out_specs=pl.BlockSpec((GROUP, 2, KB, TILE_I), lambda s: (0, 0, s, 0)),
        out_shape=jax.ShapeDtypeStruct((GROUP, 2, TILE_K, TILE_I), BF16),
        scratch_shapes=[
            pltpu.VMEM((CH, CH), BF16),
            pltpu.VMEM((TILE_K, TILE_I), F32),
            pltpu.VMEM((TILE_I * KB, CH), F32),
            pltpu.VMEM((2, 2 * GROUP * KB, 128), F32),
        ],
        compiler_params=pltpu.CompilerParams(vmem_limit_bytes=VMEM_LIMIT),
        cost_estimate=pl.CostEstimate(
            flops=2 * TILE_I * TILE_K * CH * CH, bytes_accessed=7 << 20, transcendentals=1 << 20
        ),
        name="project",
    )(pair, mask, gain, bias, lv, lg, rv, rg)


def gating_kernel(own_ref, pair_ref, gain_ref, bias_ref, weight_ref, out_ref):
    rows = pair_ref.shape[0] * pair_ref.shape[1]
    x = pair_ref[...].astype(F32)
    n = layer_norm(x, gain_ref[...].reshape(1, 1, CH), bias_ref[...].reshape(1, 1, CH))
    n = n.reshape(rows, CH).astype(BF16)
    out_ref[...] = gate(jnp.dot(n, weight_ref[...], preferred_element_type=F32))


def gating(own, pair, gain, bias, weight):
    cols = TILE_K // 4
    batch = 32
    return pl.pallas_call(
        gating_kernel,
        grid_spec=pltpu.PrefetchScalarGridSpec(
            num_scalar_prefetch=1,
            grid=(TILE_I // batch,),
            in_specs=[
                pl.BlockSpec((batch, cols, CH), lambda s, own: (s, own[0], 0)),
                pl.BlockSpec((1, CH), lambda s, own: (0, 0)),
                pl.BlockSpec((1, CH), lambda s, own: (0, 0)),
                pl.BlockSpec((CH, CH), lambda s, own: (0, 0)),
            ],
            out_specs=pl.BlockSpec((batch * cols, CH), lambda s, own: (s, 0)),
        ),
        out_shape=jax.ShapeDtypeStruct((TILE_I * cols, CH), F32),
        compiler_params=pltpu.CompilerParams(vmem_limit_bytes=VMEM_LIMIT),
        cost_estimate=pl.CostEstimate(
            flops=2 * TILE_I * cols * CH * CH, bytes_accessed=3 << 20, transcendentals=1 << 19
        ),
        name="gating",
    )(own, pair, gain, bias, weight)


def product_kernel(core_ref, left_ref, right_ref, other_ref, out_ref):
    core = core_ref[0]
    for which in range(2):
        block = (right_ref, other_ref)[which]
        right = block[...].reshape(1024, TILE_I)
        slot = core if which == 0 else 1 - core
        for z in range(2):
            left = left_ref[z].reshape(1024, TILE_I)
            out_ref[z, 0, slot] = lax.dot_general(
                right, left, (((0,), (0,)), ((), ())), preferred_element_type=F32
            ).astype(BF16)


def product(core, moved, other):
    return pl.pallas_call(
        product_kernel,
        grid_spec=pltpu.PrefetchScalarGridSpec(
            num_scalar_prefetch=1,
            grid=(2,),
            in_specs=[
                pl.BlockSpec((2, 16, 1, TILE_K, TILE_I), lambda s, core: (0, 0, 0, 0, 0)),
                pl.BlockSpec((1, 16, 1, TILE_K, TILE_I), lambda s, core: (s, 0, 1, 0, 0)),
                pl.BlockSpec((1, 16, TILE_K, TILE_I), lambda s, core: (s, 0, 0, 0)),
            ],
            out_specs=pl.BlockSpec((2, 1, 2, TILE_I, TILE_I), lambda s, core: (0, s, 0, 0, 0)),
        ),
        out_shape=jax.ShapeDtypeStruct((2, 2, 2, TILE_I, TILE_I), BF16),
        compiler_params=pltpu.CompilerParams(vmem_limit_bytes=VMEM_LIMIT),
        cost_estimate=pl.CostEstimate(flops=1 << 30, bytes_accessed=4 << 20, transcendentals=0),
        name="product",
    )(core, moved, moved, other)


def finish_kernel(prod_ref, gate_ref, gain_ref, bias_ref, weight_ref, out_ref, hidden, result):
    cols = prod_ref.shape[1]
    lanes = prod_ref.shape[2]
    batch = 8

    def add(part, sums):
        x = prod_ref[pl.ds(part * batch, batch)].astype(F32)
        return sums[0] + jnp.sum(x, axis=0), sums[1] + jnp.sum(x * x, axis=0)

    zero = jnp.zeros((cols, lanes), F32)
    first, second = lax.fori_loop(0, CH // batch, add, (zero, zero))
    mean = first * (1.0 / CH)
    scale = lax.rsqrt(second * (1.0 / CH) - mean * mean + EPS)
    for source in range(CH):
        h = (source % 4) * GROUP + source // 4
        x = prod_ref[source].astype(F32)
        hidden[pl.ds(h * cols, cols), :] = (x - mean) * scale * gain_ref[h] + bias_ref[h]
    for j in range(cols):
        rows = hidden[pl.ds(j, CH, stride=cols), :].astype(BF16)
        mixed = lax.dot_general(
            rows, weight_ref[...], (((0,), (0,)), ((), ())), preferred_element_type=F32
        )
        result[pl.ds(j, lanes, stride=cols), :] = mixed * gate_ref[pl.ds(j, lanes, stride=cols), :]
    out_ref[...] = result[...].reshape(lanes, cols, CH).astype(BF16)


def finish(prod, gates, gain, bias, weight):
    cols = TILE_K // 4
    lanes = 128
    return pl.pallas_call(
        finish_kernel,
        grid=(TILE_I // lanes,),
        in_specs=[
            pl.BlockSpec((CH, cols, lanes), lambda s: (0, 0, s)),
            pl.BlockSpec((lanes * cols, CH), lambda s: (s, 0)),
            pl.BlockSpec(memory_space=pltpu.SMEM),
            pl.BlockSpec(memory_space=pltpu.SMEM),
            pl.BlockSpec((CH, CH), lambda s: (0, 0)),
        ],
        out_specs=pl.BlockSpec((lanes, cols, CH), lambda s: (s, 0, 0)),
        out_shape=jax.ShapeDtypeStruct((TILE_I, cols, CH), BF16),
        scratch_shapes=[
            pltpu.VMEM((CH * cols, lanes), F32),
            pltpu.VMEM((lanes * cols, CH), F32),
        ],
        compiler_params=pltpu.CompilerParams(vmem_limit_bytes=VMEM_LIMIT),
        cost_estimate=pl.CostEstimate(
            flops=2 * TILE_I * cols * CH * CH, bytes_accessed=4 << 20, transcendentals=0
        ),
        name="finish",
    )(prod, gates, gain, bias, weight)


def on_device(
    pair, pair_mask, ln_gain, ln_bias, left_value, left_gate, right_value, right_gate,
    hid_gain, hid_bias, out_weight, out_gate,
):
    gain = ln_gain.reshape(1, CH)
    bias = ln_bias.reshape(1, CH)
    core = lax.axis_index("core").astype(jnp.int32).reshape(1)
    own = lax.axis_index("chan").astype(jnp.int32).reshape(1)
    sides = project(pair, pair_mask, gain, bias, left_value, left_gate, right_value, right_gate)
    moved = lax.all_to_all(sides, ("zl", "x", "y"), 0, 0, tiled=True)
    gates = gating(own, pair, gain, bias, out_gate)
    moved = moved.reshape(2, 16, 2, TILE_K, TILE_I)
    other = lax.ppermute(moved[:, :, 1], "core", [(0, 1), (1, 0)])
    prod = product(core, moved, other).reshape(CH, TILE_K // 4, TILE_I)
    prod = lax.all_to_all(prod, ("zl", "x", "y", "chan"), 0, 0, tiled=True)
    return finish(prod, gates, hid_gain, hid_bias, out_weight)


def solution(mesh):
    split = Mesh(mesh.devices.reshape(2, 2, 4, 4, 4), ("zl", "core", "x", "y", "chan"))
    row, col = ("zl", "core"), ("x", "y")
    return jax.shard_map(
        on_device,
        mesh=split,
        in_specs=(
            P(row, col, None),
            P(row, col),
            P(),
            P(),
            P(None, "chan"),
            P(None, "chan"),
            P(None, "chan"),
            P(None, "chan"),
            P(),
            P(),
            P(),
            P(),
        ),
        out_specs=P(row, ("x", "y", "chan"), None),
        check_vma=False,
    )
```

```python
import jax
import jax.numpy as jnp
from jax import lax
from jax.experimental import pallas as pl
from jax.experimental.pallas import tpu as pltpu
from jax.sharding import Mesh, PartitionSpec as P

F32 = jnp.float32
BF16 = jnp.bfloat16
EPS = 1e-05
VMEM_LIMIT = 48 * 1024 * 1024
PROJECT_LIMIT = 60 * 1024 * 1024

TILE_I = 256
TILE_K = 64
CH = 128
GROUP = 32
KB = 16
PITCH = 24


def layer_norm(x, gain, bias):
    centre = jnp.mean(x, axis=-1, keepdims=True)
    shifted = x - centre
    spread = jnp.mean(shifted * shifted, axis=-1, keepdims=True)
    return shifted * lax.rsqrt(spread + EPS) * gain + bias


def whole(*shape):
    return pl.BlockSpec(shape, lambda *s: (0,) * len(shape))


def project_kernel(
    pair_ref, mask_ref, gain_ref, bias_ref, lv_ref, lg_ref, rv_ref, rg_ref, out_ref, normed, staged
):
    step = pl.program_id(0)
    gain, bias = gain_ref[...], bias_ref[...]
    half = jnp.asarray(0.5, BF16)
    weights = jnp.concatenate([lv_ref[...], rv_ref[...], lg_ref[...], rg_ref[...]], axis=0) * half
    flat = normed.reshape(TILE_I * PITCH, CH)
    flat_staged = staged.reshape(2 * 2 * GROUP * PITCH, 128)
    batch = 64
    for part in range(TILE_I // batch):
        x = pair_ref[part * batch : (part + 1) * batch].astype(F32).reshape(batch * KB, CH)
        n = layer_norm(x, gain, bias)
        normed[part * batch : (part + 1) * batch, :KB, :] = n.reshape(batch, KB, CH)
    for k in range(KB):
        rows = flat[pl.ds(k, TILE_I, stride=PITCH), :].astype(BF16)
        y = lax.dot_general(
            weights, rows, (((1,), (1,)), ((), ())), preferred_element_type=F32
        )
        kept = mask_ref[pl.ds(step * KB + k, 1), :].astype(F32)
        sides = (jnp.tanh(y[2 * GROUP :]) + 1.0) * (y[: 2 * GROUP] * kept)
        for part in range(2):
            first = part * 2 * GROUP * PITCH + k
            flat_staged[pl.ds(first, 2 * GROUP, stride=PITCH), :] = sides[:, part * 128 : (part + 1) * 128]
    for side in range(2):
        for part in range(2):
            block = staged[part, side * GROUP : (side + 1) * GROUP, :KB, :]
            out_ref[:, side, :, part * 128 : (part + 1) * 128] = block.astype(BF16)


def project(pair, mask, gain, bias, lv, lg, rv, rg):
    return pl.pallas_call(
        project_kernel,
        grid=(TILE_K // KB,),
        in_specs=[
            pl.BlockSpec((TILE_I, KB, CH), lambda s: (0, s, 0)),
            whole(TILE_K, TILE_I),
            whole(1, CH),
            whole(1, CH),
            whole(GROUP, CH),
            whole(GROUP, CH),
            whole(GROUP, CH),
            whole(GROUP, CH),
        ],
        out_specs=pl.BlockSpec((GROUP, 2, KB, TILE_I), lambda s: (0, 0, s, 0)),
        out_shape=jax.ShapeDtypeStruct((GROUP, 2, TILE_K, TILE_I), BF16),
        scratch_shapes=[
            pltpu.VMEM((TILE_I, PITCH, CH), F32),
            pltpu.VMEM((2, 2 * GROUP, PITCH, 128), F32),
        ],
        compiler_params=pltpu.CompilerParams(vmem_limit_bytes=PROJECT_LIMIT),
        cost_estimate=pl.CostEstimate(
            flops=2 * TILE_I * TILE_K * CH * CH, bytes_accessed=7 << 20, transcendentals=1 << 20
        ),
        name="project",
    )(pair, mask, gain, bias, lv, lg, rv, rg)


def gating_kernel(own_ref, pair_ref, gain_ref, bias_ref, weight_ref, out_ref, normed):
    batch, cols, _ = pair_ref.shape
    x = pair_ref[...].astype(F32).reshape(batch * cols, CH)
    n = layer_norm(x, gain_ref[...], bias_ref[...])
    normed[:, :cols, :] = n.reshape(batch, cols, CH)
    flat = normed.reshape(batch * PITCH, CH)
    for j in range(cols):
        rows = flat[pl.ds(j, batch, stride=PITCH), :].astype(BF16)
        y = jnp.dot(rows, weight_ref[...], preferred_element_type=F32)
        out_ref[j] = 0.5 * jnp.tanh(0.5 * y) + 0.5


def gating(own, pair, gain, bias, weight):
    cols = TILE_K // 4
    batch = 64
    return pl.pallas_call(
        gating_kernel,
        grid_spec=pltpu.PrefetchScalarGridSpec(
            num_scalar_prefetch=1,
            grid=(TILE_I // batch,),
            in_specs=[
                pl.BlockSpec((batch, cols, CH), lambda s, own: (s, own[0], 0)),
                whole(1, CH),
                whole(1, CH),
                whole(CH, CH),
            ],
            out_specs=pl.BlockSpec((cols, batch, CH), lambda s, own: (0, s, 0)),
            scratch_shapes=[pltpu.VMEM((batch, PITCH, CH), F32)],
        ),
        out_shape=jax.ShapeDtypeStruct((cols, TILE_I, CH), F32),
        compiler_params=pltpu.CompilerParams(vmem_limit_bytes=VMEM_LIMIT),
        cost_estimate=pl.CostEstimate(
            flops=2 * TILE_I * cols * CH * CH, bytes_accessed=3 << 20, transcendentals=1 << 19
        ),
        name="gating",
    )(own, pair, gain, bias, weight)


def product_kernel(core_ref, left_ref, right_ref, other_ref, out_ref):
    core = core_ref[0]
    for which in range(2):
        block = (right_ref, other_ref)[which]
        right = block[...].reshape(1024, TILE_I)
        slot = core if which == 0 else 1 - core
        for z in range(2):
            left = left_ref[z].reshape(1024, TILE_I)
            out_ref[z, 0, slot] = lax.dot_general(
                right, left, (((0,), (0,)), ((), ())), preferred_element_type=F32
            ).astype(BF16)


def product(core, moved, other):
    return pl.pallas_call(
        product_kernel,
        grid_spec=pltpu.PrefetchScalarGridSpec(
            num_scalar_prefetch=1,
            grid=(2,),
            in_specs=[
                pl.BlockSpec((2, 16, 1, TILE_K, TILE_I), lambda s, core: (0, 0, 0, 0, 0)),
                pl.BlockSpec((1, 16, 1, TILE_K, TILE_I), lambda s, core: (s, 0, 1, 0, 0)),
                pl.BlockSpec((1, 16, TILE_K, TILE_I), lambda s, core: (s, 0, 0, 0)),
            ],
            out_specs=pl.BlockSpec((2, 1, 2, TILE_I, TILE_I), lambda s, core: (0, s, 0, 0, 0)),
        ),
        out_shape=jax.ShapeDtypeStruct((2, 2, 2, TILE_I, TILE_I), BF16),
        compiler_params=pltpu.CompilerParams(vmem_limit_bytes=VMEM_LIMIT),
        cost_estimate=pl.CostEstimate(flops=1 << 30, bytes_accessed=4 << 20, transcendentals=0),
        name="product",
    )(core, moved, moved, other)


def finish_kernel(prod_ref, gate_ref, gain_ref, bias_ref, weight_ref, out_ref, hidden, result):
    cols = prod_ref.shape[1]
    lanes = prod_ref.shape[2]
    batch = 8

    def add(part, sums):
        x = prod_ref[pl.ds(part * batch, batch)].astype(F32)
        return sums[0] + jnp.sum(x, axis=0), sums[1] + jnp.sum(x * x, axis=0)

    zero = jnp.zeros((cols, lanes), F32)
    first, second = lax.fori_loop(0, CH // batch, add, (zero, zero))
    mean = first * (1.0 / CH)
    scale = lax.rsqrt(second * (1.0 / CH) - mean * mean + EPS)
    flat_hidden = hidden.reshape(CH * PITCH, lanes)
    flat_result = result.reshape(lanes * PITCH, CH)
    for source in range(CH):
        h = (source % 4) * GROUP + source // 4
        x = prod_ref[source].astype(F32)
        hidden[h, :cols, :] = (x - mean) * scale * gain_ref[h] + bias_ref[h]
    for j in range(cols):
        rows = flat_hidden[pl.ds(j, CH, stride=PITCH), :].astype(BF16)
        mixed = lax.dot_general(
            rows, weight_ref[...], (((0,), (0,)), ((), ())), preferred_element_type=F32
        )
        flat_result[pl.ds(j, lanes, stride=PITCH), :] = mixed * gate_ref[j]
    out_ref[...] = result[:, :cols, :].astype(BF16)


def finish(prod, gates, gain, bias, weight):
    cols = TILE_K // 4
    lanes = 128
    return pl.pallas_call(
        finish_kernel,
        grid=(TILE_I // lanes,),
        in_specs=[
            pl.BlockSpec((CH, cols, lanes), lambda s: (0, 0, s)),
            pl.BlockSpec((cols, lanes, CH), lambda s: (0, s, 0)),
            pl.BlockSpec(memory_space=pltpu.SMEM),
            pl.BlockSpec(memory_space=pltpu.SMEM),
            pl.BlockSpec((CH, CH), lambda s: (0, 0)),
        ],
        out_specs=pl.BlockSpec((lanes, cols, CH), lambda s: (s, 0, 0)),
        out_shape=jax.ShapeDtypeStruct((TILE_I, cols, CH), BF16),
        scratch_shapes=[
            pltpu.VMEM((CH, PITCH, lanes), F32),
            pltpu.VMEM((lanes, PITCH, CH), F32),
        ],
        compiler_params=pltpu.CompilerParams(vmem_limit_bytes=VMEM_LIMIT),
        cost_estimate=pl.CostEstimate(
            flops=2 * TILE_I * cols * CH * CH, bytes_accessed=4 << 20, transcendentals=0
        ),
        name="finish",
    )(prod, gates, gain, bias, weight)


def on_device(
    pair, pair_mask, ln_gain, ln_bias, left_value, left_gate, right_value, right_gate,
    hid_gain, hid_bias, out_weight, out_gate,
):
    gain = ln_gain.reshape(1, CH)
    bias = ln_bias.reshape(1, CH)
    core = lax.axis_index("core").astype(jnp.int32).reshape(1)
    own = lax.axis_index("chan").astype(jnp.int32).reshape(1)
    sides = project(
        pair, pair_mask.T, gain, bias, left_value.T, left_gate.T, right_value.T, right_gate.T
    )
    moved = lax.all_to_all(sides, ("zl", "x", "y"), 0, 0, tiled=True)
    moved = moved.reshape(2, 16, 2, TILE_K, TILE_I)
    other = lax.ppermute(moved[:, :, 1], "core", [(0, 1), (1, 0)])
    gates = gating(own, pair, gain, bias, out_gate)
    prod = product(core, moved, other).reshape(CH, TILE_K // 4, TILE_I)
    prod = lax.all_to_all(prod, ("zl", "x", "y", "chan"), 0, 0, tiled=True)
    return finish(prod, gates, hid_gain, hid_bias, out_weight)


def solution(mesh):
    split = Mesh(mesh.devices.reshape(2, 2, 4, 4, 4), ("zl", "core", "x", "y", "chan"))
    row, col = ("zl", "core"), ("x", "y")
    return jax.shard_map(
        on_device,
        mesh=split,
        in_specs=(
            P(row, col, None),
            P(row, col),
            P(),
            P(),
            P(None, "chan"),
            P(None, "chan"),
            P(None, "chan"),
            P(None, "chan"),
            P(),
            P(),
            P(),
            P(),
        ),
        out_specs=P(row, ("x", "y", "chan"), None),
        check_vma=False,
    )
```

```python
import jax
import jax.numpy as jnp
from jax import lax
from jax.experimental import pallas as pl
from jax.experimental.pallas import tpu as pltpu
from jax.sharding import Mesh, PartitionSpec as P

F32 = jnp.float32
BF16 = jnp.bfloat16
EPS = 1e-05
VMEM_LIMIT = 48 * 1024 * 1024
PRODUCT_LIMIT = 24 * 1024 * 1024
PROJECT_LIMIT = 60 * 1024 * 1024

TILE_I = 256
TILE_K = 64
CH = 128
GROUP = 32
KB = 16
PITCH = 24


def layer_norm(x, gain, bias):
    share = jnp.full((CH, CH), 1.0 / CH, BF16)
    shifted = x.astype(F32) - jnp.dot(x, share, preferred_element_type=F32)
    spread = jnp.mean(shifted * shifted, axis=-1, keepdims=True)
    return shifted * lax.rsqrt(spread + EPS) * gain + bias


def whole(*shape):
    return pl.BlockSpec(shape, lambda *s: (0,) * len(shape))


def project_kernel(
    pair_ref, mask_ref, gain_ref, bias_ref, lv_ref, lg_ref, rv_ref, rg_ref, out_ref, normed, staged
):
    step = pl.program_id(0)
    gain, bias = gain_ref[...], bias_ref[...]
    half = jnp.asarray(0.5, BF16)
    weights = jnp.concatenate([lv_ref[...], rv_ref[...], lg_ref[...], rg_ref[...]], axis=0) * half
    flat = normed.reshape(TILE_I * PITCH, CH)
    flat_staged = staged.reshape(2 * 2 * GROUP * PITCH, 128)
    batch = 64
    for part in range(TILE_I // batch):
        x = pair_ref[part * batch : (part + 1) * batch].reshape(batch * KB, CH)
        n = layer_norm(x, gain, bias)
        normed[part * batch : (part + 1) * batch, :KB, :] = n.reshape(batch, KB, CH)
    for k in range(KB):
        rows = flat[pl.ds(k, TILE_I, stride=PITCH), :].astype(BF16)
        y = lax.dot_general(
            weights, rows, (((1,), (1,)), ((), ())), preferred_element_type=F32
        )
        kept = mask_ref[pl.ds(step * KB + k, 1), :].astype(F32)
        sides = (jnp.tanh(y[2 * GROUP :]) + 1.0) * (y[: 2 * GROUP] * kept)
        for part in range(2):
            first = part * 2 * GROUP * PITCH + k
            flat_staged[pl.ds(first, 2 * GROUP, stride=PITCH), :] = sides[:, part * 128 : (part + 1) * 128]
    for side in range(2):
        for part in range(2):
            block = staged[part, side * GROUP : (side + 1) * GROUP, :KB, :]
            out_ref[:, side, :, part * 128 : (part + 1) * 128] = block.astype(BF16)


def project(pair, mask, gain, bias, lv, lg, rv, rg):
    return pl.pallas_call(
        project_kernel,
        grid=(TILE_K // KB,),
        in_specs=[
            pl.BlockSpec((TILE_I, KB, CH), lambda s: (0, s, 0)),
            whole(TILE_K, TILE_I),
            whole(1, CH),
            whole(1, CH),
            whole(GROUP, CH),
            whole(GROUP, CH),
            whole(GROUP, CH),
            whole(GROUP, CH),
        ],
        out_specs=pl.BlockSpec((GROUP, 2, KB, TILE_I), lambda s: (0, 0, s, 0)),
        out_shape=jax.ShapeDtypeStruct((GROUP, 2, TILE_K, TILE_I), BF16),
        scratch_shapes=[
            pltpu.VMEM((TILE_I, PITCH, CH), F32),
            pltpu.VMEM((2, 2 * GROUP, PITCH, 128), F32),
        ],
        compiler_params=pltpu.CompilerParams(vmem_limit_bytes=PROJECT_LIMIT),
        cost_estimate=pl.CostEstimate(
            flops=2 * TILE_I * TILE_K * CH * CH, bytes_accessed=7 << 20, transcendentals=1 << 20
        ),
        name="project",
    )(pair, mask, gain, bias, lv, lg, rv, rg)


def gating_kernel(own_ref, pair_ref, gain_ref, bias_ref, weight_ref, out_ref, normed):
    batch, cols, _ = pair_ref.shape
    x = pair_ref[...].reshape(batch * cols, CH)
    n = layer_norm(x, gain_ref[...], bias_ref[...])
    normed[:, :cols, :] = n.reshape(batch, cols, CH)
    flat = normed.reshape(batch * PITCH, CH)
    for j in range(cols):
        rows = flat[pl.ds(j, batch, stride=PITCH), :].astype(BF16)
        y = jnp.dot(rows, weight_ref[...], preferred_element_type=F32)
        out_ref[j] = 0.5 * jnp.tanh(0.5 * y) + 0.5


def gating(own, pair, gain, bias, weight):
    cols = TILE_K // 4
    batch = 64
    return pl.pallas_call(
        gating_kernel,
        grid_spec=pltpu.PrefetchScalarGridSpec(
            num_scalar_prefetch=1,
            grid=(TILE_I // batch,),
            in_specs=[
                pl.BlockSpec((batch, cols, CH), lambda s, own: (s, own[0], 0)),
                whole(1, CH),
                whole(1, CH),
                whole(CH, CH),
            ],
            out_specs=pl.BlockSpec((cols, batch, CH), lambda s, own: (0, s, 0)),
            scratch_shapes=[pltpu.VMEM((batch, PITCH, CH), F32)],
        ),
        out_shape=jax.ShapeDtypeStruct((cols, TILE_I, CH), F32),
        compiler_params=pltpu.CompilerParams(vmem_limit_bytes=VMEM_LIMIT),
        cost_estimate=pl.CostEstimate(
            flops=2 * TILE_I * cols * CH * CH, bytes_accessed=3 << 20, transcendentals=1 << 19
        ),
        name="gating",
    )(own, pair, gain, bias, weight)


def product_kernel(slot_ref, left_ref, right_ref, *refs):
    out_ref = refs[-1]
    right = right_ref[...].reshape(1024, TILE_I)
    for z in range(2):
        left = left_ref[z].reshape(1024, TILE_I)
        out_ref[z, 0, 0] = lax.dot_general(
            right, left, (((0,), (0,)), ((), ())), preferred_element_type=F32
        ).astype(BF16)


def product(slot, moved, right, right_spec, earlier, name):
    shape = (2, 2, 2, TILE_I, TILE_I)
    return pl.pallas_call(
        product_kernel,
        grid_spec=pltpu.PrefetchScalarGridSpec(
            num_scalar_prefetch=1,
            grid=(2,),
            in_specs=[
                pl.BlockSpec((2, 16, 1, TILE_K, TILE_I), lambda s, slot: (0, 0, 0, 0, 0)),
                right_spec,
            ] + [pl.BlockSpec(memory_space=pl.ANY)] * len(earlier),
            out_specs=pl.BlockSpec((2, 1, 1, TILE_I, TILE_I), lambda s, slot: (0, s, slot[0], 0, 0)),
        ),
        out_shape=jax.ShapeDtypeStruct(shape, BF16),
        input_output_aliases={3: 0} if earlier else {},
        compiler_params=pltpu.CompilerParams(vmem_limit_bytes=PRODUCT_LIMIT),
        cost_estimate=pl.CostEstimate(flops=1 << 29, bytes_accessed=3 << 20, transcendentals=0),
        name=name,
    )(slot, moved, right, *earlier)


def finish_kernel(prod_ref, gate_ref, gain_ref, bias_ref, weight_ref, out_ref, hidden, result):
    cols = prod_ref.shape[1]
    lanes = prod_ref.shape[2]
    batch = 8

    def add(part, sums):
        x = prod_ref[pl.ds(part * batch, batch)].astype(F32)
        return sums[0] + jnp.sum(x, axis=0), sums[1] + jnp.sum(x * x, axis=0)

    zero = jnp.zeros((cols, lanes), F32)
    first, second = lax.fori_loop(0, CH // batch, add, (zero, zero))
    mean = first * (1.0 / CH)
    scale = lax.rsqrt(second * (1.0 / CH) - mean * mean + EPS)
    flat_hidden = hidden.reshape(CH * PITCH, lanes)
    flat_result = result.reshape(lanes * PITCH, CH)
    for source in range(CH):
        h = (source % 4) * GROUP + source // 4
        x = prod_ref[source].astype(F32)
        hidden[h, :cols, :] = (x - mean) * scale * gain_ref[h] + bias_ref[h]
    for j in range(cols):
        rows = flat_hidden[pl.ds(j, CH, stride=PITCH), :].astype(BF16)
        mixed = lax.dot_general(
            rows, weight_ref[...], (((0,), (0,)), ((), ())), preferred_element_type=F32
        )
        flat_result[pl.ds(j, lanes, stride=PITCH), :] = mixed * gate_ref[j]
    out_ref[...] = result[:, :cols, :].astype(BF16)


def finish(prod, gates, gain, bias, weight):
    cols = TILE_K // 4
    lanes = 128
    return pl.pallas_call(
        finish_kernel,
        grid=(TILE_I // lanes,),
        in_specs=[
            pl.BlockSpec((CH, cols, lanes), lambda s: (0, 0, s)),
            pl.BlockSpec((cols, lanes, CH), lambda s: (0, s, 0)),
            pl.BlockSpec(memory_space=pltpu.SMEM),
            pl.BlockSpec(memory_space=pltpu.SMEM),
            pl.BlockSpec((CH, CH), lambda s: (0, 0)),
        ],
        out_specs=pl.BlockSpec((lanes, cols, CH), lambda s: (s, 0, 0)),
        out_shape=jax.ShapeDtypeStruct((TILE_I, cols, CH), BF16),
        scratch_shapes=[
            pltpu.VMEM((CH, PITCH, lanes), F32),
            pltpu.VMEM((lanes, PITCH, CH), F32),
        ],
        compiler_params=pltpu.CompilerParams(vmem_limit_bytes=VMEM_LIMIT),
        cost_estimate=pl.CostEstimate(
            flops=2 * TILE_I * cols * CH * CH, bytes_accessed=4 << 20, transcendentals=0
        ),
        name="finish",
    )(prod, gates, gain, bias, weight)


def on_device(
    pair, pair_mask, ln_gain, ln_bias, left_value, left_gate, right_value, right_gate,
    hid_gain, hid_bias, out_weight, out_gate,
):
    gain = ln_gain.reshape(1, CH)
    bias = ln_bias.reshape(1, CH)
    core = lax.axis_index("core").astype(jnp.int32).reshape(1)
    own = lax.axis_index("chan").astype(jnp.int32).reshape(1)
    sides = project(
        pair, pair_mask.T, gain, bias, left_value.T, left_gate.T, right_value.T, right_gate.T
    )
    moved = lax.all_to_all(sides, ("zl", "x", "y"), 0, 0, tiled=True)
    moved = moved.reshape(2, 16, 2, TILE_K, TILE_I)
    other = lax.ppermute(moved[:, :, 1], "core", [(0, 1), (1, 0)])
    gates = gating(own, pair, gain, bias, out_gate)
    here = pl.BlockSpec((1, 16, 1, TILE_K, TILE_I), lambda s, slot: (s, 0, 1, 0, 0))
    there = pl.BlockSpec((1, 16, TILE_K, TILE_I), lambda s, slot: (s, 0, 0, 0))
    prod = product(core, moved, moved, here, (), "product_own")
    prod = product(1 - core, moved, other, there, (prod,), "product_other")
    prod = prod.reshape(CH, TILE_K // 4, TILE_I)
    prod = lax.all_to_all(prod, ("zl", "x", "y", "chan"), 0, 0, tiled=True)
    return finish(prod, gates, hid_gain, hid_bias, out_weight)


def solution(mesh):
    split = Mesh(mesh.devices.reshape(2, 2, 4, 4, 4), ("zl", "core", "x", "y", "chan"))
    row, col = ("zl", "core"), ("x", "y")
    return jax.shard_map(
        on_device,
        mesh=split,
        in_specs=(
            P(row, col, None),
            P(row, col),
            P(),
            P(),
            P(None, "chan"),
            P(None, "chan"),
            P(None, "chan"),
            P(None, "chan"),
            P(),
            P(),
            P(),
            P(),
        ),
        out_specs=P(row, ("x", "y", "chan"), None),
        check_vma=False,
    )
```

```python
import jax
import jax.numpy as jnp
from jax import lax
from jax.experimental import pallas as pl
from jax.experimental.pallas import tpu as pltpu
from jax.sharding import Mesh, PartitionSpec as P

F32 = jnp.float32
BF16 = jnp.bfloat16
EPS = 1e-05
VMEM_LIMIT = 48 * 1024 * 1024
PRODUCT_LIMIT = 24 * 1024 * 1024
PROJECT_LIMIT = 60 * 1024 * 1024

TILE_I = 256
TILE_K = 64
CH = 128
GROUP = 32
KB = 16
PITCH = 24


def layer_norm(x, gain, bias):
    share = jnp.full((CH, CH), 1.0 / CH, BF16)
    shifted = x.astype(F32) - jnp.dot(x, share, preferred_element_type=F32)
    spread = jnp.mean(shifted * shifted, axis=-1, keepdims=True)
    return shifted * lax.rsqrt(spread + EPS) * gain + bias


def whole(*shape):
    return pl.BlockSpec(shape, lambda *s: (0,) * len(shape))


def project_kernel(
    pair_ref, mask_ref, gain_ref, bias_ref, lv_ref, lg_ref, rv_ref, rg_ref, out_ref, normed, staged
):
    step = pl.program_id(0)
    gain, bias = gain_ref[...], bias_ref[...]
    half = jnp.asarray(0.5, BF16)
    weights = jnp.concatenate([lv_ref[...], rv_ref[...], lg_ref[...], rg_ref[...]], axis=0) * half
    flat = normed.reshape(TILE_I * PITCH, CH)
    flat_staged = staged.reshape(2 * 2 * GROUP * PITCH, 128)
    batch = 64
    for part in range(TILE_I // batch):
        x = pair_ref[part * batch : (part + 1) * batch].reshape(batch * KB, CH)
        n = layer_norm(x, gain, bias)
        normed[part * batch : (part + 1) * batch, :KB, :] = n.reshape(batch, KB, CH)
    for k in range(KB):
        rows = flat[pl.ds(k, TILE_I, stride=PITCH), :].astype(BF16)
        y = lax.dot_general(
            weights, rows, (((1,), (1,)), ((), ())), preferred_element_type=F32
        )
        kept = mask_ref[pl.ds(step * KB + k, 1), :].astype(F32)
        sides = (jnp.tanh(y[2 * GROUP :]) + 1.0) * (y[: 2 * GROUP] * kept)
        for part in range(2):
            first = part * 2 * GROUP * PITCH + k
            flat_staged[pl.ds(first, 2 * GROUP, stride=PITCH), :] = sides[:, part * 128 : (part + 1) * 128]
    for side in range(2):
        for part in range(2):
            block = staged[part, side * GROUP : (side + 1) * GROUP, :KB, :]
            out_ref[:, side, :, part * 128 : (part + 1) * 128] = block.astype(BF16)


def project(pair, mask, gain, bias, lv, lg, rv, rg):
    return pl.pallas_call(
        project_kernel,
        grid=(TILE_K // KB,),
        in_specs=[
            pl.BlockSpec((TILE_I, KB, CH), lambda s: (0, s, 0)),
            whole(TILE_K, TILE_I),
            whole(1, CH),
            whole(1, CH),
            whole(GROUP, CH),
            whole(GROUP, CH),
            whole(GROUP, CH),
            whole(GROUP, CH),
        ],
        out_specs=pl.BlockSpec((GROUP, 2, KB, TILE_I), lambda s: (0, 0, s, 0)),
        out_shape=jax.ShapeDtypeStruct((GROUP, 2, TILE_K, TILE_I), BF16),
        scratch_shapes=[
            pltpu.VMEM((TILE_I, PITCH, CH), F32),
            pltpu.VMEM((2, 2 * GROUP, PITCH, 128), F32),
        ],
        compiler_params=pltpu.CompilerParams(vmem_limit_bytes=PROJECT_LIMIT),
        cost_estimate=pl.CostEstimate(
            flops=2 * TILE_I * TILE_K * CH * CH, bytes_accessed=7 << 20, transcendentals=1 << 20
        ),
        name="project",
    )(pair, mask, gain, bias, lv, lg, rv, rg)


def gating_kernel(own_ref, pair_ref, gain_ref, bias_ref, weight_ref, out_ref, normed):
    batch, cols, _ = pair_ref.shape
    x = pair_ref[...].reshape(batch * cols, CH)
    n = layer_norm(x, gain_ref[...], bias_ref[...])
    normed[:, :cols, :] = n.reshape(batch, cols, CH)
    flat = normed.reshape(batch * PITCH, CH)
    for j in range(cols):
        rows = flat[pl.ds(j, batch, stride=PITCH), :].astype(BF16)
        y = jnp.dot(rows, weight_ref[...], preferred_element_type=F32)
        out_ref[j] = 0.5 * jnp.tanh(0.5 * y) + 0.5


def gating(own, pair, gain, bias, weight):
    cols = TILE_K // 4
    batch = 64
    return pl.pallas_call(
        gating_kernel,
        grid_spec=pltpu.PrefetchScalarGridSpec(
            num_scalar_prefetch=1,
            grid=(TILE_I // batch,),
            in_specs=[
                pl.BlockSpec((batch, cols, CH), lambda s, own: (s, own[0], 0)),
                whole(1, CH),
                whole(1, CH),
                whole(CH, CH),
            ],
            out_specs=pl.BlockSpec((cols, batch, CH), lambda s, own: (0, s, 0)),
            scratch_shapes=[pltpu.VMEM((batch, PITCH, CH), F32)],
        ),
        out_shape=jax.ShapeDtypeStruct((cols, TILE_I, CH), F32),
        compiler_params=pltpu.CompilerParams(vmem_limit_bytes=PROJECT_LIMIT),
        cost_estimate=pl.CostEstimate(
            flops=2 * TILE_I * cols * CH * CH, bytes_accessed=3 << 20, transcendentals=1 << 19
        ),
        name="gating",
    )(own, pair, gain, bias, weight)


def product_kernel(slot_ref, left_ref, right_ref, *refs):
    out_ref = refs[-1]
    right = right_ref[...].reshape(1024, TILE_I)
    for z in range(2):
        left = left_ref[z].reshape(1024, TILE_I)
        out_ref[z, 0, 0] = lax.dot_general(
            right, left, (((0,), (0,)), ((), ())), preferred_element_type=F32
        ).astype(BF16)


def product(slot, moved, right, right_spec, earlier, name):
    shape = (2, 2, 2, TILE_I, TILE_I)
    return pl.pallas_call(
        product_kernel,
        grid_spec=pltpu.PrefetchScalarGridSpec(
            num_scalar_prefetch=1,
            grid=(2,),
            in_specs=[
                pl.BlockSpec((2, 16, 1, TILE_K, TILE_I), lambda s, slot: (0, 0, 0, 0, 0)),
                right_spec,
            ] + [pl.BlockSpec(memory_space=pl.ANY)] * len(earlier),
            out_specs=pl.BlockSpec((2, 1, 1, TILE_I, TILE_I), lambda s, slot: (0, s, slot[0], 0, 0)),
        ),
        out_shape=jax.ShapeDtypeStruct(shape, BF16),
        input_output_aliases={3: 0} if earlier else {},
        compiler_params=pltpu.CompilerParams(vmem_limit_bytes=PRODUCT_LIMIT),
        cost_estimate=pl.CostEstimate(flops=1 << 29, bytes_accessed=3 << 20, transcendentals=0),
        name=name,
    )(slot, moved, right, *earlier)


def finish_kernel(prod_ref, gate_ref, gain_ref, bias_ref, weight_ref, out_ref, hidden, result):
    cols = prod_ref.shape[1]
    lanes = prod_ref.shape[2]
    batch = 8

    first = jnp.zeros((cols, lanes), F32)
    second = jnp.zeros((cols, lanes), F32)
    for part in range(CH // batch):
        x = prod_ref[part * batch : (part + 1) * batch].astype(F32)
        first, second = first + jnp.sum(x, axis=0), second + jnp.sum(x * x, axis=0)
    mean = first * (1.0 / CH)
    scale = lax.rsqrt(second * (1.0 / CH) - mean * mean + EPS)
    flat_hidden = hidden.reshape(CH * PITCH, lanes)
    flat_result = result.reshape(lanes * PITCH, CH)
    for source in range(CH):
        h = (source % 4) * GROUP + source // 4
        x = prod_ref[source].astype(F32)
        hidden[h, :cols, :] = (x - mean) * scale * gain_ref[h] + bias_ref[h]
    for j in range(cols):
        rows = flat_hidden[pl.ds(j, CH, stride=PITCH), :].astype(BF16)
        mixed = lax.dot_general(
            rows, weight_ref[...], (((0,), (0,)), ((), ())), preferred_element_type=F32
        )
        flat_result[pl.ds(j, lanes, stride=PITCH), :] = mixed * gate_ref[j]
    out_ref[...] = result[:, :cols, :].astype(BF16)


def finish(prod, gates, gain, bias, weight):
    cols = TILE_K // 4
    lanes = 128
    return pl.pallas_call(
        finish_kernel,
        grid=(TILE_I // lanes,),
        in_specs=[
            pl.BlockSpec((CH, cols, lanes), lambda s: (0, 0, s)),
            pl.BlockSpec((cols, lanes, CH), lambda s: (0, s, 0)),
            pl.BlockSpec(memory_space=pltpu.SMEM),
            pl.BlockSpec(memory_space=pltpu.SMEM),
            pl.BlockSpec((CH, CH), lambda s: (0, 0)),
        ],
        out_specs=pl.BlockSpec((lanes, cols, CH), lambda s: (s, 0, 0)),
        out_shape=jax.ShapeDtypeStruct((TILE_I, cols, CH), BF16),
        scratch_shapes=[
            pltpu.VMEM((CH, PITCH, lanes), F32),
            pltpu.VMEM((lanes, PITCH, CH), F32),
        ],
        compiler_params=pltpu.CompilerParams(vmem_limit_bytes=VMEM_LIMIT),
        cost_estimate=pl.CostEstimate(
            flops=2 * TILE_I * cols * CH * CH, bytes_accessed=4 << 20, transcendentals=0
        ),
        name="finish",
    )(prod, gates, gain, bias, weight)


def on_device(
    pair, pair_mask, ln_gain, ln_bias, left_value, left_gate, right_value, right_gate,
    hid_gain, hid_bias, out_weight, out_gate,
):
    gain = ln_gain.reshape(1, CH)
    bias = ln_bias.reshape(1, CH)
    core = lax.axis_index("core").astype(jnp.int32).reshape(1)
    own = lax.axis_index("chan").astype(jnp.int32).reshape(1)
    sides = project(
        pair, pair_mask.T, gain, bias, left_value.T, left_gate.T, right_value.T, right_gate.T
    )
    moved = lax.all_to_all(sides, ("zl", "x", "y"), 0, 0, tiled=True)
    gates = gating(own, pair, gain, bias, out_gate)
    moved, gates = lax.optimization_barrier((moved, gates))
    moved = moved.reshape(2, 16, 2, TILE_K, TILE_I)
    other = lax.ppermute(moved[:, :, 1], "core", [(0, 1), (1, 0)])
    here = pl.BlockSpec((1, 16, 1, TILE_K, TILE_I), lambda s, slot: (s, 0, 1, 0, 0))
    there = pl.BlockSpec((1, 16, TILE_K, TILE_I), lambda s, slot: (s, 0, 0, 0))
    prod = product(core, moved, moved, here, (), "product_own")
    prod = product(1 - core, moved, other, there, (prod,), "product_other")
    prod = prod.reshape(CH, TILE_K // 4, TILE_I)
    prod = lax.all_to_all(prod, ("zl", "x", "y", "chan"), 0, 0, tiled=True)
    return finish(prod, gates, hid_gain, hid_bias, out_weight)


def solution(mesh):
    split = Mesh(mesh.devices.reshape(2, 2, 4, 4, 4), ("zl", "core", "x", "y", "chan"))
    row, col = ("zl", "core"), ("x", "y")
    return jax.shard_map(
        on_device,
        mesh=split,
        in_specs=(
            P(row, col, None),
            P(row, col),
            P(),
            P(),
            P(None, "chan"),
            P(None, "chan"),
            P(None, "chan"),
            P(None, "chan"),
            P(),
            P(),
            P(),
            P(),
        ),
        out_specs=P(row, ("x", "y", "chan"), None),
        check_vma=False,
    )
```

```python
import jax
import jax.numpy as jnp
from jax import lax
from jax.experimental import pallas as pl
from jax.experimental.pallas import tpu as pltpu
from jax.sharding import Mesh, PartitionSpec as P

F32 = jnp.float32
BF16 = jnp.bfloat16
EPS = 1e-05
VMEM_LIMIT = 48 * 1024 * 1024
PRODUCT_LIMIT = 24 * 1024 * 1024
PROJECT_LIMIT = 60 * 1024 * 1024

TILE_I = 256
TILE_K = 64
CH = 128
GROUP = 32
KB = 16
PITCH = 24


def layer_norm(x, gain, bias):
    share = jnp.full((CH, CH), 1.0 / CH, BF16)
    shifted = x.astype(F32) - jnp.dot(x, share, preferred_element_type=F32)
    spread = jnp.mean(shifted * shifted, axis=-1, keepdims=True)
    return shifted * lax.rsqrt(spread + EPS) * gain + bias


def whole(*shape):
    return pl.BlockSpec(shape, lambda *s: (0,) * len(shape))


def project_kernel(
    pair_ref, mask_ref, gain_ref, bias_ref, lv_ref, lg_ref, rv_ref, rg_ref, out_ref, normed, staged
):
    step = pl.program_id(0)
    gain, bias = gain_ref[...], bias_ref[...]
    half = jnp.asarray(0.5, BF16)
    weights = jnp.concatenate([lv_ref[...], rv_ref[...], lg_ref[...], rg_ref[...]], axis=0) * half
    flat = normed.reshape(TILE_I * PITCH, CH)
    flat_staged = staged.reshape(2 * 2 * GROUP * PITCH, 128)
    batch = 64
    for part in range(TILE_I // batch):
        x = pair_ref[part * batch : (part + 1) * batch].reshape(batch * KB, CH)
        n = layer_norm(x, gain, bias)
        normed[part * batch : (part + 1) * batch, :KB, :] = n.reshape(batch, KB, CH)
    for k in range(KB):
        rows = flat[pl.ds(k, TILE_I, stride=PITCH), :].astype(BF16)
        y = lax.dot_general(
            weights, rows, (((1,), (1,)), ((), ())), preferred_element_type=F32
        )
        kept = mask_ref[pl.ds(step * KB + k, 1), :].astype(F32)
        sides = (jnp.tanh(y[2 * GROUP :]) + 1.0) * (y[: 2 * GROUP] * kept)
        for part in range(2):
            first = part * 2 * GROUP * PITCH + k
            flat_staged[pl.ds(first, 2 * GROUP, stride=PITCH), :] = sides[:, part * 128 : (part + 1) * 128]
    for side in range(2):
        for part in range(2):
            block = staged[part, side * GROUP : (side + 1) * GROUP, :KB, :]
            out_ref[:, side, :, part * 128 : (part + 1) * 128] = block.astype(BF16)


def project(pair, mask, gain, bias, lv, lg, rv, rg):
    return pl.pallas_call(
        project_kernel,
        grid=(TILE_K // KB,),
        in_specs=[
            pl.BlockSpec((TILE_I, KB, CH), lambda s: (0, s, 0)),
            whole(TILE_K, TILE_I),
            whole(1, CH),
            whole(1, CH),
            whole(GROUP, CH),
            whole(GROUP, CH),
            whole(GROUP, CH),
            whole(GROUP, CH),
        ],
        out_specs=pl.BlockSpec((GROUP, 2, KB, TILE_I), lambda s: (0, 0, s, 0)),
        out_shape=jax.ShapeDtypeStruct((GROUP, 2, TILE_K, TILE_I), BF16),
        scratch_shapes=[
            pltpu.VMEM((TILE_I, PITCH, CH), F32),
            pltpu.VMEM((2, 2 * GROUP, PITCH, 128), F32),
        ],
        compiler_params=pltpu.CompilerParams(vmem_limit_bytes=PROJECT_LIMIT),
        cost_estimate=pl.CostEstimate(
            flops=2 * TILE_I * TILE_K * CH * CH, bytes_accessed=7 << 20, transcendentals=1 << 20
        ),
        name="project",
    )(pair, mask, gain, bias, lv, lg, rv, rg)


def gating_kernel(own_ref, pair_ref, gain_ref, bias_ref, weight_ref, out_ref, normed):
    batch, cols, _ = pair_ref.shape
    x = pair_ref[...].reshape(batch * cols, CH)
    n = layer_norm(x, gain_ref[...], bias_ref[...])
    normed[:, :cols, :] = n.reshape(batch, cols, CH)
    flat = normed.reshape(batch * PITCH, CH)
    for j in range(cols):
        rows = flat[pl.ds(j, batch, stride=PITCH), :].astype(BF16)
        y = jnp.dot(rows, weight_ref[...], preferred_element_type=F32)
        out_ref[j] = 0.5 * jnp.tanh(0.5 * y) + 0.5


def gating(own, pair, gain, bias, weight):
    cols = TILE_K // 4
    batch = 64
    return pl.pallas_call(
        gating_kernel,
        grid_spec=pltpu.PrefetchScalarGridSpec(
            num_scalar_prefetch=1,
            grid=(TILE_I // batch,),
            in_specs=[
                pl.BlockSpec((batch, cols, CH), lambda s, own: (s, own[0], 0)),
                whole(1, CH),
                whole(1, CH),
                whole(CH, CH),
            ],
            out_specs=pl.BlockSpec((cols, batch, CH), lambda s, own: (0, s, 0)),
            scratch_shapes=[pltpu.VMEM((batch, PITCH, CH), F32)],
        ),
        out_shape=jax.ShapeDtypeStruct((cols, TILE_I, CH), F32),
        compiler_params=pltpu.CompilerParams(vmem_limit_bytes=VMEM_LIMIT),
        cost_estimate=pl.CostEstimate(
            flops=2 * TILE_I * cols * CH * CH, bytes_accessed=3 << 20, transcendentals=1 << 19
        ),
        name="gating",
    )(own, pair, gain, bias, weight)


def product_kernel(slot_ref, left_ref, right_ref, *refs):
    out_ref = refs[-1]
    right = right_ref[...].reshape(1024, TILE_I)
    for z in range(2):
        left = left_ref[z].reshape(1024, TILE_I)
        out_ref[z, 0, 0] = lax.dot_general(
            right, left, (((0,), (0,)), ((), ())), preferred_element_type=F32
        ).astype(BF16)


def product(slot, moved, right, right_spec, earlier, name):
    shape = (2, 2, 2, TILE_I, TILE_I)
    return pl.pallas_call(
        product_kernel,
        grid_spec=pltpu.PrefetchScalarGridSpec(
            num_scalar_prefetch=1,
            grid=(2,),
            in_specs=[
                pl.BlockSpec((2, 16, 1, TILE_K, TILE_I), lambda s, slot: (0, 0, 0, 0, 0)),
                right_spec,
            ] + [pl.BlockSpec(memory_space=pl.ANY)] * len(earlier),
            out_specs=pl.BlockSpec((2, 1, 1, TILE_I, TILE_I), lambda s, slot: (0, s, slot[0], 0, 0)),
        ),
        out_shape=jax.ShapeDtypeStruct(shape, BF16),
        input_output_aliases={3: 0} if earlier else {},
        compiler_params=pltpu.CompilerParams(vmem_limit_bytes=PRODUCT_LIMIT),
        cost_estimate=pl.CostEstimate(flops=1 << 29, bytes_accessed=3 << 20, transcendentals=0),
        name=name,
    )(slot, moved, right, *earlier)


def finish_kernel(prod_ref, gate_ref, gain_ref, bias_ref, weight_ref, out_ref, hidden, result):
    cols = prod_ref.shape[1]
    lanes = prod_ref.shape[2]
    batch = 8

    first = jnp.zeros((cols, lanes), F32)
    second = jnp.zeros((cols, lanes), F32)
    for part in range(CH // batch):
        x = prod_ref[part * batch : (part + 1) * batch].astype(F32)
        first, second = first + jnp.sum(x, axis=0), second + jnp.sum(x * x, axis=0)
    mean = first * (1.0 / CH)
    scale = lax.rsqrt(second * (1.0 / CH) - mean * mean + EPS)
    flat_hidden = hidden.reshape(CH * PITCH, lanes)
    flat_result = result.reshape(lanes * PITCH, CH)
    for source in range(CH):
        h = (source % 4) * GROUP + source // 4
        x = prod_ref[source].astype(F32)
        hidden[h, :cols, :] = (x - mean) * scale * gain_ref[h] + bias_ref[h]
    for j in range(cols):
        rows = flat_hidden[pl.ds(j, CH, stride=PITCH), :].astype(BF16)
        mixed = lax.dot_general(
            rows, weight_ref[...], (((0,), (0,)), ((), ())), preferred_element_type=F32
        )
        flat_result[pl.ds(j, lanes, stride=PITCH), :] = mixed * gate_ref[j]
    out_ref[...] = result[:, :cols, :].astype(BF16)


def finish(prod, gates, gain, bias, weight):
    cols = TILE_K // 4
    lanes = 128
    return pl.pallas_call(
        finish_kernel,
        grid=(TILE_I // lanes,),
        in_specs=[
            pl.BlockSpec((CH, cols, lanes), lambda s: (0, 0, s)),
            pl.BlockSpec((cols, lanes, CH), lambda s: (0, s, 0)),
            pl.BlockSpec(memory_space=pltpu.SMEM),
            pl.BlockSpec(memory_space=pltpu.SMEM),
            pl.BlockSpec((CH, CH), lambda s: (0, 0)),
        ],
        out_specs=pl.BlockSpec((lanes, cols, CH), lambda s: (s, 0, 0)),
        out_shape=jax.ShapeDtypeStruct((TILE_I, cols, CH), BF16),
        scratch_shapes=[
            pltpu.VMEM((CH, PITCH, lanes), F32),
            pltpu.VMEM((lanes, PITCH, CH), F32),
        ],
        compiler_params=pltpu.CompilerParams(vmem_limit_bytes=VMEM_LIMIT),
        cost_estimate=pl.CostEstimate(
            flops=2 * TILE_I * cols * CH * CH, bytes_accessed=4 << 20, transcendentals=0
        ),
        name="finish",
    )(prod, gates, gain, bias, weight)


def on_device(
    pair, pair_mask, ln_gain, ln_bias, left_value, left_gate, right_value, right_gate,
    hid_gain, hid_bias, out_weight, out_gate,
):
    gain = ln_gain.reshape(1, CH)
    bias = ln_bias.reshape(1, CH)
    core = lax.axis_index("core").astype(jnp.int32).reshape(1)
    own = lax.axis_index("chan").astype(jnp.int32).reshape(1)
    sides = project(
        pair, pair_mask.T, gain, bias, left_value.T, left_gate.T, right_value.T, right_gate.T
    )
    moved = lax.all_to_all(sides, ("zl", "x", "y"), 0, 0, tiled=True)
    moved = moved.reshape(2, 16, 2, TILE_K, TILE_I)
    other = lax.ppermute(moved[:, :, 1], "core", [(0, 1), (1, 0)])
    gates = gating(own, pair, gain, bias, out_gate)
    here = pl.BlockSpec((1, 16, 1, TILE_K, TILE_I), lambda s, slot: (s, 0, 1, 0, 0))
    there = pl.BlockSpec((1, 16, TILE_K, TILE_I), lambda s, slot: (s, 0, 0, 0))
    prod = product(core, moved, moved, here, (), "product_own")
    prod = product(1 - core, moved, other, there, (prod,), "product_other")
    prod = prod.reshape(CH, TILE_K // 4, TILE_I)
    prod = lax.all_to_all(prod, ("zl", "x", "y", "chan"), 0, 0, tiled=True)
    return finish(prod, gates, hid_gain, hid_bias, out_weight)


def solution(mesh):
    split = Mesh(mesh.devices.reshape(2, 2, 4, 4, 4), ("zl", "core", "x", "y", "chan"))
    row, col = ("zl", "core"), ("x", "y")
    return jax.shard_map(
        on_device,
        mesh=split,
        in_specs=(
            P(row, col, None),
            P(row, col),
            P(),
            P(),
            P(None, "chan"),
            P(None, "chan"),
            P(None, "chan"),
            P(None, "chan"),
            P(),
            P(),
            P(),
            P(),
        ),
        out_specs=P(row, ("x", "y", "chan"), None),
        check_vma=False,
    )
```
